128 devices in a mesh: slab: 8 (over y, z_hi), head: 16 (over x, z_lo, core).
Axes of the slice: x: 4, y: 4, z: 4 (z_hi: 2, z_lo: 2; z = z_hi * 2 + z_lo), core: 2. Of those that a mesh axis runs over, the one named last changes fastest.
Arguments:
- queries: bfloat16 [24576, 4096], P(('slab', 'head')), may hold values from -8 to 8
- keys: bfloat16 [24576, 4096], P(('slab', 'head')), may hold values from -8 to 8
- values: bfloat16 [24576, 4096], P(('slab', 'head')), may hold values from -6 to 6
- neighbours: int32 [64, 12], P('slab'), may hold values from 0 to 63, as said below
- counts: int32 [64], P('slab'), may hold values from 6 to 12
Outputs:
- attended: bfloat16 [24576, 4096], P(('slab', 'head'))
The draws below stay inside these ranges and needn't reach their ends.
Inputs may be any that keep to these rules, and one draw needn't show every extreme that they name: `neighbours`: for each tile, entries 0 to counts - 1 are distinct tiles whose frame, row and column tile coordinates each differ from the tile's by at most one; entry 0 is the tile itself; the remaining entries equal the tile itself.
All inputs are finite; a program needn't handle non-finite values.
Results may differ from the reference program's by a relative error of at most 0.012.
Values may be sent and summed in bfloat16 or wider, within the bound.
A program may use at most 128 MiB of HBM per device.

```python
import jax
import jax.numpy as jnp
from jax import lax

HD = 128
TILES_H = 2
TILES_W = 4
NB = 12
HEADS = 32
TILE = 384
TIME_TILES = 8
TILES = 64
TOKENS = 24576


def tile_windows(key):
    tile_count = TIME_TILES * TILES_H * TILES_W
    column = jnp.arange(27, dtype=jnp.int32)
    offset_t = column // 9 - 1
    offset_h = column // 3 % 3 - 1
    offset_w = column % 3 - 1
    tile_index = jnp.arange(tile_count, dtype=jnp.int32)
    tile_t = tile_index // (TILES_H * TILES_W)
    tile_h = tile_index // TILES_W % TILES_H
    tile_w = tile_index % TILES_W
    cand_t = tile_t[:, None] + offset_t[None, :]
    cand_h = tile_h[:, None] + offset_h[None, :]
    cand_w = tile_w[:, None] + offset_w[None, :]
    inside = (cand_t >= 0) & (cand_t < TIME_TILES) & (cand_h >= 0) & (cand_h < TILES_H) & (cand_w >= 0) & (cand_w < TILES_W)
    candidate = (cand_t * TILES_H + cand_h) * TILES_W + cand_w
    scores = jax.random.randint(jax.random.fold_in(key, 201), (tile_count, 27), 0, 1 << 20) * 32 + column[None, :]
    scores = jnp.where(column[None, :] == 13, -1, scores)
    scores = jnp.where(inside, scores, scores + (1 << 26))
    ranked = jnp.argsort(scores, axis=1)
    chosen = jnp.take_along_axis(candidate, ranked[:, :NB], axis=1)
    available = jnp.sum(inside.astype(jnp.int32), axis=1)
    fewest = max(1, NB // 2)
    wanted = jax.random.randint(jax.random.fold_in(key, 202), (tile_count,), fewest, NB + 1)
    fullest = (TILES_H + min(1, TILES_H - 1)) * TILES_W + min(1, TILES_W - 1)
    window_size = jnp.where(tile_index == fullest, NB, jnp.minimum(wanted, available))
    window_size = jnp.where(tile_index == 0, fewest, window_size)
    slot_index = jnp.arange(NB, dtype=jnp.int32)
    listed = jnp.where(slot_index[None, :] < window_size[:, None], chosen, tile_index[:, None])
    return (listed.astype(jnp.int32), window_size.astype(jnp.int32))


def draw_neighbours(key, part):
    shared = tile_windows(key)
    return shared[0]


def draw_counts(key, part):
    shared = tile_windows(key)
    return shared[1]


def draw_queries(key, part):
    key = jax.random.fold_in(key, 13)
    return jnp.clip(jax.random.normal(key, (TOKENS, HEADS * HD), jnp.float32), -6.0, 6.0).astype(jnp.bfloat16)


def draw_keys(key, part):
    key = jax.random.fold_in(key, 14)
    return jnp.clip(jax.random.normal(key, (TOKENS, HEADS * HD), jnp.float32), -6.0, 6.0).astype(jnp.bfloat16)


def levels(own_key, shape, shards, low, high):
    gain = 1.0
    for axis_at, shards_of in shards:
        steps = jax.random.uniform(jax.random.fold_in(jax.random.fold_in(own_key, 6), axis_at), (shards_of,), jnp.float32, low / len(shards), high / len(shards))
        gain = gain * jnp.repeat(jnp.exp(steps), shape[axis_at] // shards_of).reshape((-1,) + (1,) * (len(shape) - 1 - axis_at))
    return gain


def noise(key, extent, width, limit, pieces=(), kind=jnp.bfloat16):
    level = levels(key, extent, pieces, -0.22, 0.18) if pieces else 1.0
    values = jax.random.normal(key, extent, jnp.float32) * width * level
    return jnp.minimum(jnp.maximum(values, -limit), limit).astype(kind)


def setup_inputs(seed: int = 0) -> dict:
    seeds = jax.random.split(jax.random.key(seed), 6)
    queries = draw_queries(jax.random.fold_in(seeds[5], 71), 0)
    keys = draw_keys(jax.random.fold_in(seeds[5], 71), 0)
    values = noise(seeds[2], (TOKENS, HEADS * HD), 1.0, 6.0, ((0, 128),))
    neighbours = draw_neighbours(jax.random.fold_in(seeds[5], 71), 0)
    counts = draw_counts(jax.random.fold_in(seeds[5], 71), 0)
    return dict(queries=queries, keys=keys, values=values, neighbours=neighbours, counts=counts)


def attend_block(query_tile, keyset, valueset, live_tiles):
    scores = jnp.einsum('qhd,khd->hqk', query_tile.astype(jnp.float32), keyset.astype(jnp.float32)) * (HD ** -0.5)
    live = (jnp.arange(keyset.shape[0], dtype=jnp.int32) // TILE) < live_tiles
    masked = jnp.where(live[None, None, :], scores, -jnp.inf)
    row_top = jnp.max(masked, axis=2, keepdims=True)
    weights_raw = jnp.where(live[None, None, :], jnp.exp(masked - row_top), 0.0)
    denominator = jnp.sum(weights_raw, axis=2, keepdims=True)
    weights = (weights_raw / denominator).astype(jnp.bfloat16)
    blended = jnp.einsum('hqk,khd->qhd', weights.astype(jnp.float32), valueset.astype(jnp.float32))
    return blended.astype(jnp.bfloat16)


def reference(queries, keys, values, neighbours, counts):
    query_tiles = queries.reshape(TILES, TILE, HEADS, HD)
    key_tiles = keys.reshape(TILES, TILE, HEADS, HD)
    value_tiles = values.reshape(TILES, TILE, HEADS, HD)

    def one_tile(inputs):
        query_tile, listed, live_tiles = inputs
        keyset = key_tiles[listed].reshape(NB * TILE, HEADS, HD)
        valueset = value_tiles[listed].reshape(NB * TILE, HEADS, HD)
        return attend_block(query_tile, keyset, valueset, live_tiles)

    blended = lax.map(one_tile, (query_tiles, neighbours, counts))
    return blended.reshape(TOKENS, HEADS * HD)
```

```python
import functools
import math

import jax
import jax.numpy as jnp
from jax import lax
from jax.experimental import pallas as pl
from jax.experimental.pallas import tpu as pltpu
from jax.sharding import PartitionSpec as P

HD = 128
TILE = 384
HALF = TILE // 2
NB = 12
MESH = pl.DeviceIdType.MESH
SCALE = math.log2(math.e) / math.sqrt(HD)


def kernel(
    q_in, k_in, v_in, ints_in, out,
    kv0, kv1, q, o, s_buf, ints_v, ints_s,
    kv_recv, q_recv, send, fwd_recv, fwd_send, o_send, o_recv, int_recv, int_send, smem_sem,
):
    kv = (kv0, kv1)
    slab = lax.axis_index("slab")
    head = lax.axis_index("head")
    y, zh = slab // 2, slab % 2
    x, zl, core = head // 4, (head // 2) % 2, head % 2
    z = zh * 2 + zl
    frame = 2 * y + core
    pair = x * 4 + z

    def worker(wx, wz, wy, wcore):
        return (wy * 2 + wz // 2, (wx * 2 + wz % 2) * 2 + wcore)

    def is_me(where):
        return (where[0] == slab) & (where[1] == head)

    def step_dest(k):
        dx = k % 4
        dz = (k // 4 + dx) % 4
        return (x + dx) % 4, (z + dz) % 4

    up_y, up_core = (frame + 1) // 2, (frame + 1) % 2
    down_y, down_core = (frame + 1) // 2 - 1, (frame + 1) % 2
    up_dev = worker(x, z, up_y, up_core)
    down_dev = worker(x, z, down_y, down_core)
    has_up = frame < 7
    has_down = frame > 0

    barrier = pltpu.get_barrier_semaphore()

    def greet(k, count):
        wx, wz = step_dest(k)
        dest = worker(wx, wz, y, zh)
        source = (y * 2 + core, k)

        @pl.when(jnp.logical_not(is_me(dest)))
        def _():
            pl.semaphore_signal(barrier, inc=1, device_id=dest, device_id_type=MESH)

        @pl.when(jnp.logical_not(is_me(source)))
        def _():
            pl.semaphore_signal(barrier, inc=1, device_id=source, device_id_type=MESH)

        return count

    lax.fori_loop(0, 16, greet, 0)

    @pl.when(has_up)
    def _():
        pl.semaphore_signal(barrier, inc=1, device_id=up_dev, device_id_type=MESH)

    @pl.when(has_down)
    def _():
        pl.semaphore_signal(barrier, inc=1, device_id=down_dev, device_id_type=MESH)

    own = jnp.where(zh == core, 2, 0)
    pl.semaphore_wait(barrier, 32 - own + has_up.astype(jnp.int32) + has_down.astype(jnp.int32))

    partner = worker(x, core * 2 + zl, y, zh)

    @pl.when(zh == core)
    def _():
        pltpu.make_async_copy(ints_in, ints_v, int_recv).start()

    @pl.when(zh != core)
    def _():
        pltpu.make_async_remote_copy(
            ints_in, ints_v, int_send, int_recv, device_id=partner, device_id_type=MESH
        ).start()

    my_tile, my_row = head // 2, pl.multiple_of(core * HALF, HALF)

    def exchange(h, k, which):
        wx, wz = step_dest(k)
        dest = worker(wx, wz, y, zh)
        col = pl.multiple_of((wx * 4 + wz) * 256 + h * 128, 128)
        src_of = (q_in, k_in, v_in)
        for a in which:
            src = src_of[a].at[:, pl.ds(col, 128)]
            if a == 0:
                dst = q.at[h, my_tile, pl.ds(my_row, HALF), :]
                sem = q_recv.at[h]
            else:
                dst = kv[h].at[a - 1, 8 + my_tile, pl.ds(my_row, HALF), :]
                sem = kv_recv.at[h, head]

            @pl.when(is_me(dest))
            def _():
                pltpu.make_async_copy(src, dst, sem).start()

            @pl.when(jnp.logical_not(is_me(dest)))
            def _():
                pltpu.make_async_remote_copy(
                    src, dst, send.at[h, k], sem, device_id=dest, device_id_type=MESH
                ).start()

    def send_all(h, which):
        def body(k, carry):
            exchange(h, k, which)
            return carry

        lax.fori_loop(0, 16, body, 0)

    for h in range(2):
        send_all(h, (1, 2))
        send_all(h, (0,))

    def forward(h, k):
        dx = k % 4
        dz = (k // 4 + dx) % 4
        sx, sz = (x + 4 - dx) % 4, (z + 4 - dz) % 4

        @pl.when(sz // 2 == core)
        def _():
            for c in range(2):
                tile = sx * 2 + sz % 2
                src = kv[h].at[:, 8 + tile, pl.ds(c * HALF, HALF), :]
                pltpu.make_async_copy(src, src, kv_recv.at[h, tile * 2 + c]).wait()

                @pl.when(has_up)
                def _():
                    pltpu.make_async_remote_copy(
                        src, kv[h].at[:, tile, pl.ds(c * HALF, HALF), :],
                        fwd_send.at[h, 0], fwd_recv.at[h, 0], device_id=up_dev, device_id_type=MESH,
                    ).start()

                @pl.when(has_down)
                def _():
                    pltpu.make_async_remote_copy(
                        src, kv[h].at[:, 16 + tile, pl.ds(c * HALF, HALF), :],
                        fwd_send.at[h, 1], fwd_recv.at[h, 1], device_id=down_dev, device_id_type=MESH,
                    ).start()

    def forward_body(k, carry):
        forward(0, k)
        return carry

    lax.fori_loop(0, 16, forward_body, 0)

    pltpu.make_async_copy(ints_v, ints_v, int_recv).wait()
    to_smem = pltpu.make_async_copy(ints_v, ints_s, smem_sem)
    to_smem.start()
    to_smem.wait()

    def arrived(h):
        pltpu.make_async_copy(q.at[h], q.at[h], q_recv.at[h]).wait()

        @pl.when(has_down)
        def _():
            part = kv[h].at[:, pl.ds(0, 8)]
            pltpu.make_async_copy(part, part, fwd_recv.at[h, 0]).wait()

        @pl.when(has_up)
        def _():
            part = kv[h].at[:, pl.ds(16, 8)]
            pltpu.make_async_copy(part, part, fwd_recv.at[h, 1]).wait()

    def attend(h, a):
        qf = q[h, a].astype(jnp.float32) * SCALE
        hi = qf.astype(jnp.bfloat16)
        lo = (qf - hi.astype(jnp.float32)).astype(jnp.bfloat16)
        q2 = jnp.concatenate([hi, lo], axis=1)
        base = 8 * (frame - 1)
        index = [jnp.clip(ints_s[a, s] - base, 0, 23) for s in range(NB)]
        count = ints_s[a, NB]
        top = None
        for p in range(NB // 2):
            keys = jnp.concatenate([kv[h][0, index[2 * p]], kv[h][0, index[2 * p + 1]]], axis=0)
            keys2 = jnp.concatenate([keys, keys], axis=1)
            s = lax.dot_general(q2, keys2, (((1,), (1,)), ((), ())), preferred_element_type=jnp.float32)
            s_buf[p] = s
            m = s[:, 0:128]
            for c in range(1, 6):
                m = jnp.maximum(m, s[:, c * 128:(c + 1) * 128])
            top = m if top is None else jnp.maximum(top, m)
        row_top = jnp.max(top, axis=1, keepdims=True)
        acc = jnp.zeros((TILE, 256), jnp.float32)
        for p in range(NB // 2):
            w = jnp.exp2(s_buf[p] - row_top).astype(jnp.bfloat16)
            vals = []
            for s in (2 * p, 2 * p + 1):
                v = kv[h][1, index[s]]
                one = jnp.ones((TILE, 128), jnp.bfloat16)
                if s >= 6:
                    live = s < count
                    v = jnp.where(live, v, jnp.zeros_like(v))
                    one = jnp.where(live, one, jnp.zeros_like(one))
                vals.append(jnp.concatenate([v, one], axis=1))
            acc += jnp.dot(w, jnp.concatenate(vals, axis=0), preferred_element_type=jnp.float32)
        o[h, a] = (acc[:, :128] / acc[:, 128:]).astype(jnp.bfloat16)

    def o_target(a, half):
        return (y * 2 + core, 2 * a + half)

    def o_copy(h, a, half):
        col = pl.multiple_of((pair * 2 + h) * 128, 128)
        src = o.at[h, a, pl.ds(half * HALF, HALF), :]
        return src, out.at[:, pl.ds(col, 128)]

    def item(h, a, carry):
        i = h * 8 + a
        if h == 0:
            forward(1, 2 * a)
            forward(1, 2 * a + 1)
        attend(h, a)
        for half in range(2):
            dest = o_target(a, half)
            src, dst = o_copy(h, a, half)

            @pl.when(is_me(dest))
            def _():
                pltpu.make_async_copy(src, dst, o_recv).start()

            @pl.when(jnp.logical_not(is_me(dest)))
            def _():
                pltpu.make_async_remote_copy(
                    src, dst, o_send.at[i * 2 + half], o_recv, device_id=dest, device_id_type=MESH
                ).start()

        return carry

    for h in range(2):
        arrived(h)
        lax.fori_loop(0, 8, functools.partial(item, h), 0)

    def finish(k, carry):
        wx, wz = step_dest(k)

        @pl.when(jnp.logical_not(is_me(worker(wx, wz, y, zh))))
        def _():
            for h in range(2):
                part = q.at[h, pl.ds(0, 3), pl.ds(0, HALF), :]
                pltpu.make_async_copy(part, part, send.at[h, k]).wait()

        for half in range(2):
            a = k % 8

            @pl.when(jnp.logical_not(is_me(o_target(a, half))))
            def _():
                part = o.at[0, 0, pl.ds(0, HALF), :]
                pltpu.make_async_copy(part, part, o_send.at[k * 2 + half]).wait()

        return carry

    lax.fori_loop(0, 16, finish, 0)
    for h in range(2):
        part = kv[h].at[:, pl.ds(0, 8)]

        @pl.when(has_up)
        def _():
            pltpu.make_async_copy(part, part, fwd_send.at[h, 0]).wait()

        @pl.when(has_down)
        def _():
            pltpu.make_async_copy(part, part, fwd_send.at[h, 1]).wait()

    @pl.when(zh != core)
    def _():
        pltpu.make_async_copy(ints_v, ints_v, int_send).wait()

    pltpu.make_async_copy(out, out, o_recv).wait()


def body(queries, keys, values, neighbours, counts):
    ints = jnp.pad(jnp.concatenate([neighbours, counts[:, None]], axis=1), ((0, 0), (0, 128 - NB - 1)))
    any_space = pl.BlockSpec(memory_space=pl.ANY)
    dma = pltpu.SemaphoreType.DMA
    return pl.pallas_call(
        kernel,
        out_shape=jax.ShapeDtypeStruct(queries.shape, queries.dtype),
        in_specs=[any_space] * 4,
        out_specs=any_space,
        scratch_shapes=[
            pltpu.VMEM((2, 24, TILE, HD), jnp.bfloat16),
            pltpu.VMEM((2, 24, TILE, HD), jnp.bfloat16),
            pltpu.VMEM((2, 8, TILE, HD), jnp.bfloat16),
            pltpu.VMEM((2, 8, TILE, HD), jnp.bfloat16),
            pltpu.VMEM((NB // 2, TILE, 2 * TILE), jnp.float32),
            pltpu.VMEM((8, 128), jnp.int32),
            pltpu.SMEM((8, 128), jnp.int32),
            dma((2, 16)),
            dma((2,)),
            dma((2, 16)),
            dma((2, 2)),
            dma((2, 2)),
            dma((32,)),
            dma,
            dma,
            dma,
            dma,
        ],
        compiler_params=pltpu.CompilerParams(
            collective_id=0, has_side_effects=True, vmem_limit_bytes=56 * 1024 * 1024
        ),
    )(queries, keys, values, ints)


def solution(mesh):
    placed = (
        P(("slab", "head"), None),
        P(("slab", "head"), None),
        P(("slab", "head"), None),
        P("slab", None),
        P("slab"),
    )
    return jax.shard_map(
        body, mesh=mesh, in_specs=placed, out_specs=P(("slab", "head"), None), check_vma=False
    )
```

```python
import functools
import math

import jax
import jax.numpy as jnp
from jax import lax
from jax.experimental import pallas as pl
from jax.experimental.pallas import tpu as pltpu
from jax.sharding import PartitionSpec as P

HD = 128
TILE = 384
HALF = TILE // 2
NB = 12
MESH = pl.DeviceIdType.MESH
SCALE = math.log2(math.e) / math.sqrt(HD)


def kernel(
    q_in, k_in, v_in, ints_in, out,
    kv0, kv1, q, o, s_even, s_odd, top_even, top_odd, ints_v, ints_s,
    kv_recv, q_recv, send, fwd_recv, fwd_send, o_send, o_recv, int_recv, int_send, smem_sem,
):
    kv = (kv0, kv1)
    slab = lax.axis_index("slab")
    head = lax.axis_index("head")
    y, zh = slab // 2, slab % 2
    x, zl, core = head // 4, (head // 2) % 2, head % 2
    z = zh * 2 + zl
    frame = 2 * y + core
    pair = x * 4 + z

    def worker(wx, wz, wy, wcore):
        return (wy * 2 + wz // 2, (wx * 2 + wz % 2) * 2 + wcore)

    def is_me(where):
        return (where[0] == slab) & (where[1] == head)

    def step_dest(k):
        dx = k % 4
        dz = (k // 4 + dx) % 4
        return (x + dx) % 4, (z + dz) % 4

    up_y, up_core = (frame + 1) // 2, (frame + 1) % 2
    down_y, down_core = (frame + 1) // 2 - 1, (frame + 1) % 2
    up_dev = worker(x, z, up_y, up_core)
    down_dev = worker(x, z, down_y, down_core)
    has_up = frame < 7
    has_down = frame > 0

    barrier = pltpu.get_barrier_semaphore()

    def greet(k, count):
        wx, wz = step_dest(k)
        dest = worker(wx, wz, y, zh)
        source = (y * 2 + core, k)

        @pl.when(jnp.logical_not(is_me(dest)))
        def _():
            pl.semaphore_signal(barrier, inc=1, device_id=dest, device_id_type=MESH)

        @pl.when(jnp.logical_not(is_me(source)))
        def _():
            pl.semaphore_signal(barrier, inc=1, device_id=source, device_id_type=MESH)

        return count

    lax.fori_loop(0, 16, greet, 0)

    @pl.when(has_up)
    def _():
        pl.semaphore_signal(barrier, inc=1, device_id=up_dev, device_id_type=MESH)

    @pl.when(has_down)
    def _():
        pl.semaphore_signal(barrier, inc=1, device_id=down_dev, device_id_type=MESH)

    own = jnp.where(zh == core, 2, 0)
    pl.semaphore_wait(barrier, 32 - own + has_up.astype(jnp.int32) + has_down.astype(jnp.int32))

    partner = worker(x, core * 2 + zl, y, zh)

    @pl.when(zh == core)
    def _():
        pltpu.make_async_copy(ints_in, ints_v, int_recv).start()

    @pl.when(zh != core)
    def _():
        pltpu.make_async_remote_copy(
            ints_in, ints_v, int_send, int_recv, device_id=partner, device_id_type=MESH
        ).start()

    my_tile, my_row = head // 2, pl.multiple_of(core * HALF, HALF)

    def exchange(h, k, which):
        wx, wz = step_dest(k)
        dest = worker(wx, wz, y, zh)
        col = pl.multiple_of((wx * 4 + wz) * 256 + h * 128, 128)
        src_of = (q_in, k_in, v_in)
        for a in which:
            src = src_of[a].at[:, pl.ds(col, 128)]
            if a == 0:
                dst = q.at[h, my_tile, pl.ds(my_row, HALF), :]
                sem = q_recv.at[h]
            else:
                dst = kv[h].at[a - 1, 8 + my_tile, pl.ds(my_row, HALF), :]
                sem = kv_recv.at[h, head]

            @pl.when(is_me(dest))
            def _():
                pltpu.make_async_copy(src, dst, sem).start()

            @pl.when(jnp.logical_not(is_me(dest)))
            def _():
                pltpu.make_async_remote_copy(
                    src, dst, send.at[h, k], sem, device_id=dest, device_id_type=MESH
                ).start()

    def send_all(h, which):
        def body(k, carry):
            exchange(h, k, which)
            return carry

        lax.fori_loop(0, 16, body, 0)

    for h in range(2):
        send_all(h, (1, 2))
        send_all(h, (0,))

    def forward(h, k):
        dx = k % 4
        dz = (k // 4 + dx) % 4
        sx, sz = (x + 4 - dx) % 4, (z + 4 - dz) % 4

        @pl.when(sz // 2 == core)
        def _():
            for c in range(2):
                tile = sx * 2 + sz % 2
                src = kv[h].at[:, 8 + tile, pl.ds(c * HALF, HALF), :]
                pltpu.make_async_copy(src, src, kv_recv.at[h, tile * 2 + c]).wait()

                @pl.when(has_up)
                def _():
                    pltpu.make_async_remote_copy(
                        src, kv[h].at[:, tile, pl.ds(c * HALF, HALF), :],
                        fwd_send.at[h, 0], fwd_recv.at[h, 0], device_id=up_dev, device_id_type=MESH,
                    ).start()

                @pl.when(has_down)
                def _():
                    pltpu.make_async_remote_copy(
                        src, kv[h].at[:, 16 + tile, pl.ds(c * HALF, HALF), :],
                        fwd_send.at[h, 1], fwd_recv.at[h, 1], device_id=down_dev, device_id_type=MESH,
                    ).start()

    def forward_body(k, carry):
        forward(0, k)
        return carry

    lax.fori_loop(0, 16, forward_body, 0)

    pltpu.make_async_copy(ints_v, ints_v, int_recv).wait()
    to_smem = pltpu.make_async_copy(ints_v, ints_s, smem_sem)
    to_smem.start()
    to_smem.wait()

    def arrived(h):
        pltpu.make_async_copy(q.at[h], q.at[h], q_recv.at[h]).wait()

        @pl.when(has_down)
        def _():
            part = kv[h].at[:, pl.ds(0, 8)]
            pltpu.make_async_copy(part, part, fwd_recv.at[h, 0]).wait()

        @pl.when(has_up)
        def _():
            part = kv[h].at[:, pl.ds(16, 8)]
            pltpu.make_async_copy(part, part, fwd_recv.at[h, 1]).wait()

    base = 8 * (frame - 1)

    def tiles_of(a):
        return [jnp.clip(ints_s[a, s] - base, 0, 23) for s in range(NB)]

    def score(h, a, p, index, s_ref, top):
        keys = jnp.concatenate([kv[h][0, index[2 * p]], kv[h][0, index[2 * p + 1]]], axis=0)
        s = lax.dot_general(q[h, a], keys, (((1,), (1,)), ((), ())), preferred_element_type=jnp.float32)
        s_ref[p] = s
        for c in range(6):
            m = s[:, c * 128:(c + 1) * 128]
            top = m if top is None else jnp.maximum(top, m)
        return top

    def keep_top(top, top_ref):
        top_ref[...] = jnp.broadcast_to(jnp.max(top, axis=1, keepdims=True), (TILE, 128))

    def blend(h, a, p, index, s_ref, row_top):
        w = jnp.exp2((s_ref[p] - row_top) * SCALE).astype(jnp.bfloat16)
        vals = []
        for s in (2 * p, 2 * p + 1):
            v = kv[h][1, index[s]]
            one = jnp.ones((TILE, 128), jnp.bfloat16)
            if s >= 6:
                live = ints_s[a, s] != ints_s[a, 0]
                v = jnp.where(live, v, jnp.zeros_like(v))
                one = jnp.where(live, one, jnp.zeros_like(one))
            vals.append(jnp.concatenate([v, one], axis=1))
        return jnp.dot(w, jnp.concatenate(vals, axis=0), preferred_element_type=jnp.float32)

    def attend(h, a, cur, nxt):
        index = tiles_of(a)
        row_top = cur[1][:, 0:1]
        total, top = None, None
        if nxt is not None:
            index_next = tiles_of(a + 1)
        for p in range(NB // 2):
            if nxt is not None:
                top = score(h, a + 1, p, index_next, nxt[0], top)
            part = blend(h, a, p, index, cur[0], row_top)
            total = part if total is None else total + part
        if nxt is not None:
            keep_top(top, nxt[1])
        o[h, a] = (total[:, :128] / total[:, 128:]).astype(jnp.bfloat16)

    def o_target(a, half):
        return (y * 2 + core, 2 * a + half)

    def o_copy(h, a, half):
        col = pl.multiple_of((pair * 2 + h) * 128, 128)
        src = o.at[h, a, pl.ds(half * HALF, HALF), :]
        return src, out.at[:, pl.ds(col, 128)]

    even, odd = (s_even, top_even), (s_odd, top_odd)

    def item(h, a, cur, nxt):
        i = h * 8 + a
        if h == 0:
            forward(1, 2 * a)
            forward(1, 2 * a + 1)
        attend(h, a, cur, nxt)
        for half in range(2):
            dest = o_target(a, half)
            src, dst = o_copy(h, a, half)

            @pl.when(is_me(dest))
            def _():
                pltpu.make_async_copy(src, dst, o_recv).start()

            @pl.when(jnp.logical_not(is_me(dest)))
            def _():
                pltpu.make_async_remote_copy(
                    src, dst, o_send.at[i * 2 + half], o_recv, device_id=dest, device_id_type=MESH
                ).start()

    for h in range(2):
        arrived(h)
        first, top = tiles_of(0), None
        for p in range(NB // 2):
            top = score(h, 0, p, first, s_even, top)
        keep_top(top, top_even)

        def two(j, carry):
            item(h, 2 * j, even, odd)
            item(h, 2 * j + 1, odd, even)
            return carry

        lax.fori_loop(0, 3, two, 0)
        item(h, 6, even, odd)
        item(h, 7, odd, None)

    def finish(k, carry):
        wx, wz = step_dest(k)

        @pl.when(jnp.logical_not(is_me(worker(wx, wz, y, zh))))
        def _():
            for h in range(2):
                part = q.at[h, pl.ds(0, 3), pl.ds(0, HALF), :]
                pltpu.make_async_copy(part, part, send.at[h, k]).wait()

        for half in range(2):
            a = k % 8

            @pl.when(jnp.logical_not(is_me(o_target(a, half))))
            def _():
                part = o.at[0, 0, pl.ds(0, HALF), :]
                pltpu.make_async_copy(part, part, o_send.at[k * 2 + half]).wait()

        return carry

    lax.fori_loop(0, 16, finish, 0)
    for h in range(2):
        part = kv[h].at[:, pl.ds(0, 8)]

        @pl.when(has_up)
        def _():
            pltpu.make_async_copy(part, part, fwd_send.at[h, 0]).wait()

        @pl.when(has_down)
        def _():
            pltpu.make_async_copy(part, part, fwd_send.at[h, 1]).wait()

    @pl.when(zh != core)
    def _():
        pltpu.make_async_copy(ints_v, ints_v, int_send).wait()

    pltpu.make_async_copy(out, out, o_recv).wait()


def body(queries, keys, values, neighbours, counts):
    any_space = pl.BlockSpec(memory_space=pl.ANY)
    dma = pltpu.SemaphoreType.DMA
    return pl.pallas_call(
        kernel,
        out_shape=jax.ShapeDtypeStruct(queries.shape, queries.dtype),
        in_specs=[any_space] * 4,
        out_specs=any_space,
        scratch_shapes=[
            pltpu.VMEM((2, 24, TILE, HD), jnp.bfloat16),
            pltpu.VMEM((2, 24, TILE, HD), jnp.bfloat16),
            pltpu.VMEM((2, 8, TILE, HD), jnp.bfloat16),
            pltpu.VMEM((2, 8, TILE, HD), jnp.bfloat16),
            pltpu.VMEM((NB // 2, TILE, 2 * TILE), jnp.float32),
            pltpu.VMEM((NB // 2, TILE, 2 * TILE), jnp.float32),
            pltpu.VMEM((TILE, 128), jnp.float32),
            pltpu.VMEM((TILE, 128), jnp.float32),
            pltpu.VMEM((8, NB), jnp.int32),
            pltpu.SMEM((8, NB), jnp.int32),
            dma((2, 16)),
            dma((2,)),
            dma((2, 16)),
            dma((2, 2)),
            dma((2, 2)),
            dma((32,)),
            dma,
            dma,
            dma,
            dma,
        ],
        compiler_params=pltpu.CompilerParams(
            collective_id=0, has_side_effects=True, vmem_limit_bytes=56 * 1024 * 1024
        ),
    )(queries, keys, values, neighbours)


def solution(mesh):
    placed = (
        P(("slab", "head"), None),
        P(("slab", "head"), None),
        P(("slab", "head"), None),
        P("slab", None),
        P("slab"),
    )
    return jax.shard_map(
        body, mesh=mesh, in_specs=placed, out_specs=P(("slab", "head"), None), check_vma=False
    )
```

```python
import functools
import math

import jax
import jax.numpy as jnp
from jax import lax
from jax.experimental import pallas as pl
from jax.experimental.pallas import tpu as pltpu
from jax.sharding import PartitionSpec as P

HD = 128
TILE = 384
HALF = TILE // 2
NB = 12
MESH = pl.DeviceIdType.MESH
SCALE = math.log2(math.e) / math.sqrt(HD)


def kernel(
    q_in, k_in, v_in, ints_in, out,
    kv0, kv1, q, o, s_even, s_odd, top_even, top_odd, ints_v, ints_s,
    kv_recv, q_recv, send, fwd_recv, fwd_send, o_send, o_recv, int_recv, int_send, smem_sem,
):
    kv = (kv0, kv1)
    slab = lax.axis_index("slab")
    head = lax.axis_index("head")
    y, zh = slab // 2, slab % 2
    x, zl, core = head // 4, (head // 2) % 2, head % 2
    z = zh * 2 + zl
    frame = 2 * y + core
    pair = x * 4 + z

    def worker(wx, wz, wy, wcore):
        return (wy * 2 + wz // 2, (wx * 2 + wz % 2) * 2 + wcore)

    def is_me(where):
        return (where[0] == slab) & (where[1] == head)

    def step_dest(k):
        dx = k % 4
        dz = (k // 4 + dx) % 4
        return (x + dx) % 4, (z + dz) % 4

    up_y, up_core = (frame + 1) // 2, (frame + 1) % 2
    down_y, down_core = (frame + 1) // 2 - 1, (frame + 1) % 2
    up_dev = worker(x, z, up_y, up_core)
    down_dev = worker(x, z, down_y, down_core)
    has_up = frame < 7
    has_down = frame > 0

    barrier = pltpu.get_barrier_semaphore()

    def greet(k, count):
        wx, wz = step_dest(k)
        dest = worker(wx, wz, y, zh)
        source = (y * 2 + core, k)

        @pl.when(jnp.logical_not(is_me(dest)))
        def _():
            pl.semaphore_signal(barrier, inc=1, device_id=dest, device_id_type=MESH)

        @pl.when(jnp.logical_not(is_me(source)))
        def _():
            pl.semaphore_signal(barrier, inc=1, device_id=source, device_id_type=MESH)

        return count

    lax.fori_loop(0, 16, greet, 0)

    @pl.when(has_up)
    def _():
        pl.semaphore_signal(barrier, inc=1, device_id=up_dev, device_id_type=MESH)

    @pl.when(has_down)
    def _():
        pl.semaphore_signal(barrier, inc=1, device_id=down_dev, device_id_type=MESH)

    own = jnp.where(zh == core, 2, 0)
    pl.semaphore_wait(barrier, 32 - own + has_up.astype(jnp.int32) + has_down.astype(jnp.int32))

    partner = worker(x, core * 2 + zl, y, zh)

    @pl.when(zh == core)
    def _():
        pltpu.make_async_copy(ints_in, ints_v, int_recv).start()

    @pl.when(zh != core)
    def _():
        pltpu.make_async_remote_copy(
            ints_in, ints_v, int_send, int_recv, device_id=partner, device_id_type=MESH
        ).start()

    my_tile, my_row = head // 2, pl.multiple_of(core * HALF, HALF)

    def exchange(h, k, which):
        wx, wz = step_dest(k)
        dest = worker(wx, wz, y, zh)
        col = pl.multiple_of((wx * 4 + wz) * 256 + h * 128, 128)
        src_of = (q_in, k_in, v_in)
        for a in which:
            src = src_of[a].at[:, pl.ds(col, 128)]
            if a == 0:
                dst = q.at[h, my_tile, pl.ds(my_row, HALF), :]
                sem = q_recv.at[h, my_tile]
            else:
                dst = kv[h].at[a - 1, 8 + my_tile, pl.ds(my_row, HALF), :]
                sem = kv_recv.at[h, head]

            @pl.when(is_me(dest))
            def _():
                pltpu.make_async_copy(src, dst, sem).start()

            @pl.when(jnp.logical_not(is_me(dest)))
            def _():
                pltpu.make_async_remote_copy(
                    src, dst, send.at[h, k], sem, device_id=dest, device_id_type=MESH
                ).start()

    def send_all(h, which):
        def body(k, carry):
            exchange(h, k, which)
            return carry

        lax.fori_loop(0, 16, body, 0)

    for h in range(2):
        send_all(h, (1, 2))
        send_all(h, (0,))

    def forward(h, k):
        dx = k % 4
        dz = (k // 4 + dx) % 4
        sx, sz = (x + 4 - dx) % 4, (z + 4 - dz) % 4

        @pl.when(sz // 2 == core)
        def _():
            for c in range(2):
                tile = sx * 2 + sz % 2
                src = kv[h].at[:, 8 + tile, pl.ds(c * HALF, HALF), :]
                pltpu.make_async_copy(src, src, kv_recv.at[h, tile * 2 + c]).wait()

                @pl.when(has_up)
                def _():
                    pltpu.make_async_remote_copy(
                        src, kv[h].at[:, tile, pl.ds(c * HALF, HALF), :],
                        fwd_send.at[h, 0], fwd_recv.at[h, 0], device_id=up_dev, device_id_type=MESH,
                    ).start()

                @pl.when(has_down)
                def _():
                    pltpu.make_async_remote_copy(
                        src, kv[h].at[:, 16 + tile, pl.ds(c * HALF, HALF), :],
                        fwd_send.at[h, 1], fwd_recv.at[h, 1], device_id=down_dev, device_id_type=MESH,
                    ).start()

    def forward_body(h, k, carry):
        forward(h, k)
        return carry

    lax.fori_loop(0, 16, functools.partial(forward_body, 0), 0)

    pltpu.make_async_copy(ints_v, ints_v, int_recv).wait()
    to_smem = pltpu.make_async_copy(ints_v, ints_s, smem_sem)
    to_smem.start()
    to_smem.wait()

    def tile_at(n):
        side = 1 - n % 2
        dx = (z + 8 - n // 2 - 2 * core - side) % 4
        return ((x + 4 - dx) % 4) * 2 + side

    def query_arrived(h, a):
        pltpu.make_async_copy(q.at[h, a], q.at[h, a], q_recv.at[h, a]).wait()

    def arrived(h):
        @pl.when(has_down)
        def _():
            part = kv[h].at[:, pl.ds(0, 8)]
            pltpu.make_async_copy(part, part, fwd_recv.at[h, 0]).wait()

        @pl.when(has_up)
        def _():
            part = kv[h].at[:, pl.ds(16, 8)]
            pltpu.make_async_copy(part, part, fwd_recv.at[h, 1]).wait()

    base = 8 * (frame - 1)

    def tiles_of(a):
        return [jnp.clip(ints_s[a, s] - base, 0, 23) for s in range(NB)]

    def score(h, a, p, index, s_ref, top):
        keys = jnp.concatenate([kv[h][0, index[2 * p]], kv[h][0, index[2 * p + 1]]], axis=0)
        s = lax.dot_general(q[h, a], keys, (((1,), (1,)), ((), ())), preferred_element_type=jnp.float32)
        s_ref[p] = s
        for c in range(6):
            m = s[:, c * 128:(c + 1) * 128]
            top = m if top is None else jnp.maximum(top, m)
        return top

    def keep_top(top, top_ref):
        top_ref[...] = jnp.broadcast_to(jnp.max(top, axis=1, keepdims=True), (TILE, 128))

    def blend(h, a, p, index, s_ref, row_top):
        w = jnp.exp2((s_ref[p] - row_top) * SCALE).astype(jnp.bfloat16)
        vals = []
        for s in (2 * p, 2 * p + 1):
            v = kv[h][1, index[s]]
            one = jnp.ones((TILE, 128), jnp.bfloat16)
            if s >= 6:
                live = ints_s[a, s] != ints_s[a, 0]
                v = jnp.where(live, v, jnp.zeros_like(v))
                one = jnp.where(live, one, jnp.zeros_like(one))
            vals.append(jnp.concatenate([v, one], axis=1))
        return jnp.dot(w, jnp.concatenate(vals, axis=0), preferred_element_type=jnp.float32)

    def attend(h, n, cur, nxt):
        a = tile_at(n)
        index = tiles_of(a)
        row_top = cur[1][:, 0:1]
        total, top = None, None
        if nxt is not None:
            after = tile_at(n + 1)
            query_arrived(h, after)
            index_next = tiles_of(after)
        for p in range(NB // 2):
            if nxt is not None:
                top = score(h, after, p, index_next, nxt[0], top)
            part = blend(h, a, p, index, cur[0], row_top)
            total = part if total is None else total + part
        if nxt is not None:
            keep_top(top, nxt[1])
        o[h, a] = (total[:, :128] / total[:, 128:]).astype(jnp.bfloat16)

    def o_target(a, half):
        return (y * 2 + core, 2 * a + half)

    def o_copy(h, a, half):
        col = pl.multiple_of((pair * 2 + h) * 128, 128)
        src = o.at[h, a, pl.ds(half * HALF, HALF), :]
        return src, out.at[:, pl.ds(col, 128)]

    even, odd = (s_even, top_even), (s_odd, top_odd)

    def item(h, n, cur, nxt):
        if h == 0:

            @pl.when(n >= 2)
            def _():
                forward(1, 2 * n - 4)
                forward(1, 2 * n - 3)

        if h == 1:

            @pl.when(n < 4)
            def _():
                give(0, tile_at(2 * n))
                give(0, tile_at(2 * n + 1))

        attend(h, n, cur, nxt)
        if h == 1:
            give(1, tile_at(n))

    def give(h, a):
        for half in range(2):
            dest = o_target(a, half)
            src, dst = o_copy(h, a, half)

            @pl.when(is_me(dest))
            def _():
                pltpu.make_async_copy(src, dst, o_recv).start()

            @pl.when(jnp.logical_not(is_me(dest)))
            def _():
                pltpu.make_async_remote_copy(
                    src, dst, o_send.at[h * 16 + a * 2 + half], o_recv, device_id=dest, device_id_type=MESH
                ).start()

    for h in range(2):
        if h == 1:
            lax.fori_loop(12, 16, functools.partial(forward_body, 1), 0)
        arrived(h)
        first, top = tile_at(0), None
        query_arrived(h, first)
        index_first = tiles_of(first)
        for p in range(NB // 2):
            top = score(h, first, p, index_first, s_even, top)
        keep_top(top, top_even)

        def two(j, carry):
            item(h, 2 * j, even, odd)
            item(h, 2 * j + 1, odd, even)
            return carry

        lax.fori_loop(0, 3, two, 0)
        item(h, 6, even, odd)
        item(h, 7, odd, None)

    def finish(k, carry):
        wx, wz = step_dest(k)

        @pl.when(jnp.logical_not(is_me(worker(wx, wz, y, zh))))
        def _():
            for h in range(2):
                part = q.at[h, pl.ds(0, 3), pl.ds(0, HALF), :]
                pltpu.make_async_copy(part, part, send.at[h, k]).wait()

        for half in range(2):
            a = k % 8

            @pl.when(jnp.logical_not(is_me(o_target(a, half))))
            def _():
                part = o.at[0, 0, pl.ds(0, HALF), :]
                pltpu.make_async_copy(part, part, o_send.at[k * 2 + half]).wait()

        return carry

    lax.fori_loop(0, 16, finish, 0)
    for h in range(2):
        part = kv[h].at[:, pl.ds(0, 8)]

        @pl.when(has_up)
        def _():
            pltpu.make_async_copy(part, part, fwd_send.at[h, 0]).wait()

        @pl.when(has_down)
        def _():
            pltpu.make_async_copy(part, part, fwd_send.at[h, 1]).wait()

    @pl.when(zh != core)
    def _():
        pltpu.make_async_copy(ints_v, ints_v, int_send).wait()

    pltpu.make_async_copy(out, out, o_recv).wait()


def body(queries, keys, values, neighbours, counts):
    any_space = pl.BlockSpec(memory_space=pl.ANY)
    dma = pltpu.SemaphoreType.DMA
    return settle(pl.pallas_call(
        kernel,
        out_shape=jax.ShapeDtypeStruct(queries.shape, queries.dtype),
        in_specs=[any_space] * 4,
        out_specs=any_space,
        scratch_shapes=[
            pltpu.VMEM((2, 24, TILE, HD), jnp.bfloat16),
            pltpu.VMEM((2, 24, TILE, HD), jnp.bfloat16),
            pltpu.VMEM((2, 8, TILE, HD), jnp.bfloat16),
            pltpu.VMEM((2, 8, TILE, HD), jnp.bfloat16),
            pltpu.VMEM((NB // 2, TILE, 2 * TILE), jnp.float32),
            pltpu.VMEM((NB // 2, TILE, 2 * TILE), jnp.float32),
            pltpu.VMEM((TILE, 128), jnp.float32),
            pltpu.VMEM((TILE, 128), jnp.float32),
            pltpu.VMEM((8, NB), jnp.int32),
            pltpu.SMEM((8, NB), jnp.int32),
            dma((2, 16)),
            dma((2, 8)),
            dma((2, 16)),
            dma((2, 2)),
            dma((2, 2)),
            dma((32,)),
            dma,
            dma,
            dma,
            dma,
        ],
        compiler_params=pltpu.CompilerParams(
            collective_id=0, has_side_effects=True, vmem_limit_bytes=56 * 1024 * 1024
        ),
    )(queries, keys, values, neighbours))


def settle(result):
    def copy(src, dst, held, into, outof):
        reads = [
            pltpu.make_async_copy(src.at[pl.ds(i * 48, 48)], held.at[pl.ds(i * 48, 48)], into.at[i]) for i in range(4)
        ]
        writes = [
            pltpu.make_async_copy(held.at[pl.ds(i * 48, 48)], dst.at[pl.ds(i * 48, 48)], outof.at[i]) for i in range(4)
        ]
        for c in reads:
            c.start()
        for r, c in zip(reads, writes):
            r.wait()
            c.start()
        for c in writes:
            c.wait()

    return pl.pallas_call(
        copy,
        out_shape=jax.ShapeDtypeStruct(result.shape, result.dtype),
        in_specs=[pl.BlockSpec(memory_space=pl.ANY)],
        out_specs=pl.BlockSpec(memory_space=pl.ANY),
        scratch_shapes=[
            pltpu.VMEM(result.shape, result.dtype), pltpu.SemaphoreType.DMA((4,)), pltpu.SemaphoreType.DMA((4,))
        ],
    )(result)


def solution(mesh):
    placed = (
        P(("slab", "head"), None),
        P(("slab", "head"), None),
        P(("slab", "head"), None),
        P("slab", None),
        P("slab"),
    )
    return jax.shard_map(
        body, mesh=mesh, in_specs=placed, out_specs=P(("slab", "head"), None), check_vma=False
    )
```

```python
import functools
import math

import jax
import jax.numpy as jnp
from jax import lax
from jax.experimental import pallas as pl
from jax.experimental.pallas import tpu as pltpu
from jax.sharding import PartitionSpec as P

HD = 128
TILE = 384
HALF = TILE // 2
NB = 12
MESH = pl.DeviceIdType.MESH
SCALE = math.log2(math.e) / math.sqrt(HD)


def kernel(
    q_in, k_in, v_in, ints_in, out,
    kv0, kv1, q, o, s_even, s_odd, top_even, top_odd, ints_v, ints_s,
    kv_recv, q_recv, send, fwd_recv, fwd_send, o_send, o_recv, int_recv, int_send, smem_sem,
):
    kv = (kv0, kv1)
    slab = lax.axis_index("slab")
    head = lax.axis_index("head")
    y, zh = slab // 2, slab % 2
    x, zl, core = head // 4, (head // 2) % 2, head % 2
    z = zh * 2 + zl
    frame = 2 * y + core
    pair = x * 4 + z

    def worker(wx, wz, wy, wcore):
        return (wy * 2 + wz // 2, (wx * 2 + wz % 2) * 2 + wcore)

    def is_me(where):
        return (where[0] == slab) & (where[1] == head)

    def step_dest(k):
        dx = k % 4
        dz = (k // 4 + 4 - dx) % 4
        return (x + dx) % 4, (z + dz) % 4

    up_y, up_core = (frame + 1) // 2, (frame + 1) % 2
    down_y, down_core = (frame + 1) // 2 - 1, (frame + 1) % 2
    up_dev = worker(x, z, up_y, up_core)
    down_dev = worker(x, z, down_y, down_core)
    has_up = frame < 7
    has_down = frame > 0

    barrier = pltpu.get_barrier_semaphore()

    def greet(k, count):
        wx, wz = step_dest(k)
        dest = worker(wx, wz, y, zh)
        source = (y * 2 + core, k)

        @pl.when(jnp.logical_not(is_me(dest)))
        def _():
            pl.semaphore_signal(barrier, inc=1, device_id=dest, device_id_type=MESH)

        @pl.when(jnp.logical_not(is_me(source)))
        def _():
            pl.semaphore_signal(barrier, inc=1, device_id=source, device_id_type=MESH)

        return count

    lax.fori_loop(0, 16, greet, 0)

    @pl.when(has_up)
    def _():
        pl.semaphore_signal(barrier, inc=1, device_id=up_dev, device_id_type=MESH)

    @pl.when(has_down)
    def _():
        pl.semaphore_signal(barrier, inc=1, device_id=down_dev, device_id_type=MESH)

    own = jnp.where(zh == core, 2, 0)
    pl.semaphore_wait(barrier, 32 - own + has_up.astype(jnp.int32) + has_down.astype(jnp.int32))

    partner = worker(x, core * 2 + zl, y, zh)

    @pl.when(zh == core)
    def _():
        pltpu.make_async_copy(ints_in, ints_v, int_recv).start()

    @pl.when(zh != core)
    def _():
        pltpu.make_async_remote_copy(
            ints_in, ints_v, int_send, int_recv, device_id=partner, device_id_type=MESH
        ).start()

    my_tile, my_row = head // 2, pl.multiple_of(core * HALF, HALF)

    def exchange(h, k, which):
        wx, wz = step_dest(k)
        dest = worker(wx, wz, y, zh)
        col = pl.multiple_of((wx * 4 + wz) * 256 + h * 128, 128)
        src_of = (q_in, k_in, v_in)
        for a in which:
            src = src_of[a].at[:, pl.ds(col, 128)]
            if a == 0:
                dst = q.at[h, my_tile, pl.ds(my_row, HALF), :]
                sem = q_recv.at[h, my_tile]
            else:
                dst = kv[h].at[a - 1, 8 + my_tile, pl.ds(my_row, HALF), :]
                sem = kv_recv.at[h, head]

            @pl.when(is_me(dest))
            def _():
                pltpu.make_async_copy(src, dst, sem).start()

            @pl.when(jnp.logical_not(is_me(dest)))
            def _():
                pltpu.make_async_remote_copy(
                    src, dst, send.at[h, k], sem, device_id=dest, device_id_type=MESH
                ).start()

    def send_all(h, which, first=0, last=16):
        def body(k, carry):
            exchange(h, k, which)
            return carry

        lax.fori_loop(first, last, body, 0)

    send_all(0, (1, 2))
    send_all(0, (0,), 0, 12)
    send_all(1, (1, 2))
    send_all(0, (0,), 12, 16)
    send_all(1, (0,))

    def forward(h, k):
        dx = k % 4
        dz = (k // 4 + 4 - dx) % 4
        sx, sz = (x + 4 - dx) % 4, (z + 4 - dz) % 4

        @pl.when(sz // 2 == core)
        def _():
            for c in range(2):
                tile = sx * 2 + sz % 2
                src = kv[h].at[:, 8 + tile, pl.ds(c * HALF, HALF), :]
                pltpu.make_async_copy(src, src, kv_recv.at[h, tile * 2 + c]).wait()

                @pl.when(has_up)
                def _():
                    pltpu.make_async_remote_copy(
                        src, kv[h].at[:, tile, pl.ds(c * HALF, HALF), :],
                        fwd_send.at[h, 0], fwd_recv.at[h, 0], device_id=up_dev, device_id_type=MESH,
                    ).start()

                @pl.when(has_down)
                def _():
                    pltpu.make_async_remote_copy(
                        src, kv[h].at[:, 16 + tile, pl.ds(c * HALF, HALF), :],
                        fwd_send.at[h, 1], fwd_recv.at[h, 1], device_id=down_dev, device_id_type=MESH,
                    ).start()

    def forward_body(h, k, carry):
        forward(h, k)
        return carry

    lax.fori_loop(0, 16, functools.partial(forward_body, 0), 0)

    pltpu.make_async_copy(ints_v, ints_v, int_recv).wait()
    to_smem = pltpu.make_async_copy(ints_v, ints_s, smem_sem)
    to_smem.start()
    to_smem.wait()

    def tile_at(n):
        side = 1 - n % 2
        dx = (2 * core + side + n // 2 + 4 - z) % 4
        return ((x + 4 - dx) % 4) * 2 + side

    def query_arrived(h, a):
        pltpu.make_async_copy(q.at[h, a], q.at[h, a], q_recv.at[h, a]).wait()

    def arrived(h):
        @pl.when(has_down)
        def _():
            part = kv[h].at[:, pl.ds(0, 8)]
            pltpu.make_async_copy(part, part, fwd_recv.at[h, 0]).wait()

        @pl.when(has_up)
        def _():
            part = kv[h].at[:, pl.ds(16, 8)]
            pltpu.make_async_copy(part, part, fwd_recv.at[h, 1]).wait()

    base = 8 * (frame - 1)

    def tiles_of(a):
        return [jnp.clip(ints_s[a, s] - base, 0, 23) for s in range(NB)]

    def score(h, a, p, index, s_ref, top):
        keys = jnp.concatenate([kv[h][0, index[2 * p]], kv[h][0, index[2 * p + 1]]], axis=0)
        halves = [
            lax.dot_general(
                q[h, a, i * HALF:(i + 1) * HALF], keys, (((1,), (1,)), ((), ())), preferred_element_type=jnp.float32
            )
            for i in range(2)
        ]
        s = jnp.concatenate(halves, axis=0)
        s_ref[p] = s
        for c in range(6):
            m = s[:, c * 128:(c + 1) * 128]
            top = m if top is None else jnp.maximum(top, m)
        return top

    def keep_top(top, top_ref):
        top_ref[...] = jnp.broadcast_to(jnp.max(top, axis=1, keepdims=True), (TILE, 128))

    def blend(h, a, p, index, s_ref, row_top):
        w = jnp.exp2((s_ref[p] - row_top) * SCALE).astype(jnp.bfloat16)
        vals = []
        for s in (2 * p, 2 * p + 1):
            v = kv[h][1, index[s]]
            one = jnp.ones((TILE, 128), jnp.bfloat16)
            if s >= 6:
                live = ints_s[a, s] != ints_s[a, 0]
                v = jnp.where(live, v, jnp.zeros_like(v))
                one = jnp.where(live, one, jnp.zeros_like(one))
            vals.append(jnp.concatenate([v, one], axis=1))
        return jnp.dot(w, jnp.concatenate(vals, axis=0), preferred_element_type=jnp.float32)

    def attend(h, n, cur, nxt):
        a = tile_at(n)
        index = tiles_of(a)
        row_top = cur[1][:, 0:1]
        total, top = None, None
        if nxt is not None:
            after = tile_at(n + 1)
            query_arrived(h, after)
            index_next = tiles_of(after)
        for p in range(NB // 2):
            if nxt is not None:
                top = score(h, after, p, index_next, nxt[0], top)
            part = blend(h, a, p, index, cur[0], row_top)
            total = part if total is None else total + part
        if nxt is not None:
            keep_top(top, nxt[1])
        o[h, a] = (total[:, :128] / total[:, 128:]).astype(jnp.bfloat16)

    def o_target(a, half):
        return (y * 2 + core, 2 * a + half)

    def o_copy(h, a, half):
        col = pl.multiple_of((pair * 2 + h) * 128, 128)
        src = o.at[h, a, pl.ds(half * HALF, HALF), :]
        return src, out.at[:, pl.ds(col, 128)]

    even, odd = (s_even, top_even), (s_odd, top_odd)

    def item(h, n, cur, nxt):
        if h == 0:

            @pl.when((n >= 2) & (n <= 5))
            def _():
                start = jnp.where(n == 2, 0, 2 * n - 2)
                stop = jnp.where(n == 5, 16, 2 * n)
                lax.fori_loop(start, stop, functools.partial(forward_body, 1), 0)

        if h == 1:

            @pl.when(n < 4)
            def _():
                give(0, tile_at(2 * n))
                give(0, tile_at(2 * n + 1))

        attend(h, n, cur, nxt)
        if h == 1:
            give(1, tile_at(n))

    def give(h, a):
        for half in range(2):
            dest = o_target(a, half)
            src, dst = o_copy(h, a, half)

            @pl.when(is_me(dest))
            def _():
                pltpu.make_async_copy(src, dst, o_recv).start()

            @pl.when(jnp.logical_not(is_me(dest)))
            def _():
                pltpu.make_async_remote_copy(
                    src, dst, o_send.at[h * 16 + a * 2 + half], o_recv, device_id=dest, device_id_type=MESH
                ).start()

    for h in range(2):
        arrived(h)
        first, top = tile_at(0), None
        query_arrived(h, first)
        index_first = tiles_of(first)
        for p in range(NB // 2):
            top = score(h, first, p, index_first, s_even, top)
        keep_top(top, top_even)

        def two(j, carry):
            item(h, 2 * j, even, odd)
            item(h, 2 * j + 1, odd, even)
            return carry

        lax.fori_loop(0, 3, two, 0)
        item(h, 6, even, odd)
        item(h, 7, odd, None)

    def finish(k, carry):
        wx, wz = step_dest(k)

        @pl.when(jnp.logical_not(is_me(worker(wx, wz, y, zh))))
        def _():
            for h in range(2):
                part = q.at[h, pl.ds(0, 3), pl.ds(0, HALF), :]
                pltpu.make_async_copy(part, part, send.at[h, k]).wait()

        for half in range(2):
            a = k % 8

            @pl.when(jnp.logical_not(is_me(o_target(a, half))))
            def _():
                part = o.at[0, 0, pl.ds(0, HALF), :]
                pltpu.make_async_copy(part, part, o_send.at[k * 2 + half]).wait()

        return carry

    lax.fori_loop(0, 16, finish, 0)
    for h in range(2):
        part = kv[h].at[:, pl.ds(0, 8)]

        @pl.when(has_up)
        def _():
            pltpu.make_async_copy(part, part, fwd_send.at[h, 0]).wait()

        @pl.when(has_down)
        def _():
            pltpu.make_async_copy(part, part, fwd_send.at[h, 1]).wait()

    @pl.when(zh != core)
    def _():
        pltpu.make_async_copy(ints_v, ints_v, int_send).wait()

    pltpu.make_async_copy(out, out, o_recv).wait()


def body(queries, keys, values, neighbours, counts):
    any_space = pl.BlockSpec(memory_space=pl.ANY)
    dma = pltpu.SemaphoreType.DMA
    return settle(pl.pallas_call(
        kernel,
        out_shape=jax.ShapeDtypeStruct(queries.shape, queries.dtype),
        in_specs=[any_space] * 4,
        out_specs=any_space,
        scratch_shapes=[
            pltpu.VMEM((2, 24, TILE, HD), jnp.bfloat16),
            pltpu.VMEM((2, 24, TILE, HD), jnp.bfloat16),
            pltpu.VMEM((2, 8, TILE, HD), jnp.bfloat16),
            pltpu.VMEM((2, 8, TILE, HD), jnp.bfloat16),
            pltpu.VMEM((NB // 2, TILE, 2 * TILE), jnp.float32),
            pltpu.VMEM((NB // 2, TILE, 2 * TILE), jnp.float32),
            pltpu.VMEM((TILE, 128), jnp.float32),
            pltpu.VMEM((TILE, 128), jnp.float32),
            pltpu.VMEM((8, NB), jnp.int32),
            pltpu.SMEM((8, NB), jnp.int32),
            dma((2, 16)),
            dma((2, 8)),
            dma((2, 16)),
            dma((2, 2)),
            dma((2, 2)),
            dma((32,)),
            dma,
            dma,
            dma,
            dma,
        ],
        compiler_params=pltpu.CompilerParams(
            collective_id=0, has_side_effects=True, vmem_limit_bytes=56 * 1024 * 1024
        ),
    )(queries, keys, values, neighbours))


def settle(result):
    def copy(src, dst, held, into, outof):
        reads = [
            pltpu.make_async_copy(src.at[pl.ds(i * 48, 48)], held.at[pl.ds(i * 48, 48)], into.at[i]) for i in range(4)
        ]
        writes = [
            pltpu.make_async_copy(held.at[pl.ds(i * 48, 48)], dst.at[pl.ds(i * 48, 48)], outof.at[i]) for i in range(4)
        ]
        for c in reads:
            c.start()
        for r, c in zip(reads, writes):
            r.wait()
            c.start()
        for c in writes:
            c.wait()

    return pl.pallas_call(
        copy,
        out_shape=jax.ShapeDtypeStruct(result.shape, result.dtype),
        in_specs=[pl.BlockSpec(memory_space=pl.ANY)],
        out_specs=pl.BlockSpec(memory_space=pl.ANY),
        scratch_shapes=[
            pltpu.VMEM(result.shape, result.dtype), pltpu.SemaphoreType.DMA((4,)), pltpu.SemaphoreType.DMA((4,))
        ],
    )(result)


def solution(mesh):
    placed = (
        P(("slab", "head"), None),
        P(("slab", "head"), None),
        P(("slab", "head"), None),
        P("slab", None),
        P("slab"),
    )
    return jax.shard_map(
        body, mesh=mesh, in_specs=placed, out_specs=P(("slab", "head"), None), check_vma=False
    )
```

```python
import functools
import math

import jax
import jax.numpy as jnp
from jax import lax
from jax.experimental import pallas as pl
from jax.experimental.pallas import tpu as pltpu
from jax.sharding import PartitionSpec as P

HD = 128
TILE = 384
HALF = TILE // 2
NB = 12
MESH = pl.DeviceIdType.MESH
SCALE = math.log2(math.e) / math.sqrt(HD)


def kernel(
    q_in, k_in, v_in, ints_in, out,
    kv0, kv1, q, o, s_even, s_odd, top_even, top_odd, ints_v, ints_s,
    kv_recv, q_recv, send, fwd_recv, fwd_send, o_send, o_recv, int_recv, int_send, smem_sem,
):
    kv = (kv0, kv1)
    slab = lax.axis_index("slab")
    head = lax.axis_index("head")
    y, zh = slab // 2, slab % 2
    x, zl, core = head // 4, (head // 2) % 2, head % 2
    z = zh * 2 + zl
    frame = 2 * y + core
    pair = x * 4 + z

    def worker(wx, wz, wy, wcore):
        return (wy * 2 + wz // 2, (wx * 2 + wz % 2) * 2 + wcore)

    def is_me(where):
        return (where[0] == slab) & (where[1] == head)

    def step_dest(k):
        dx = k % 4
        dz = (k // 4 + 4 - dx) % 4
        return (x + dx) % 4, (z + dz) % 4

    up_y, up_core = (frame + 1) // 2, (frame + 1) % 2
    down_y, down_core = (frame + 1) // 2 - 1, (frame + 1) % 2
    up_dev = worker(x, z, up_y, up_core)
    down_dev = worker(x, z, down_y, down_core)
    has_up = frame < 7
    has_down = frame > 0

    barrier = pltpu.get_barrier_semaphore()

    def greet(k, count):
        wx, wz = step_dest(k)
        dest = worker(wx, wz, y, zh)
        source = (y * 2 + core, k)

        @pl.when(jnp.logical_not(is_me(dest)))
        def _():
            pl.semaphore_signal(barrier, inc=1, device_id=dest, device_id_type=MESH)

        @pl.when(jnp.logical_not(is_me(source)))
        def _():
            pl.semaphore_signal(barrier, inc=1, device_id=source, device_id_type=MESH)

        return count

    lax.fori_loop(0, 16, greet, 0)

    @pl.when(has_up)
    def _():
        pl.semaphore_signal(barrier, inc=1, device_id=up_dev, device_id_type=MESH)

    @pl.when(has_down)
    def _():
        pl.semaphore_signal(barrier, inc=1, device_id=down_dev, device_id_type=MESH)

    own = jnp.where(zh == core, 2, 0)
    pl.semaphore_wait(barrier, 32 - own + has_up.astype(jnp.int32) + has_down.astype(jnp.int32))

    partner = worker(x, core * 2 + zl, y, zh)

    @pl.when(zh == core)
    def _():
        pltpu.make_async_copy(ints_in, ints_v, int_recv).start()

    @pl.when(zh != core)
    def _():
        pltpu.make_async_remote_copy(
            ints_in, ints_v, int_send, int_recv, device_id=partner, device_id_type=MESH
        ).start()

    my_tile, my_row = head // 2, pl.multiple_of(core * HALF, HALF)

    def exchange(h, k, which):
        wx, wz = step_dest(k)
        dest = worker(wx, wz, y, zh)
        col = pl.multiple_of((wx * 4 + wz) * 256 + h * 128, 128)
        src_of = (q_in, k_in, v_in)
        for a in which:
            src = src_of[a].at[:, pl.ds(col, 128)]
            if a == 0:
                dst = q.at[h, my_tile, pl.ds(my_row, HALF), :]
                sem = q_recv.at[h, my_tile]
            else:
                dst = kv[h].at[a - 1, 8 + my_tile, pl.ds(my_row, HALF), :]
                sem = kv_recv.at[h, head]

            @pl.when(is_me(dest))
            def _():
                pltpu.make_async_copy(src, dst, sem).start()

            @pl.when(jnp.logical_not(is_me(dest)))
            def _():
                pltpu.make_async_remote_copy(
                    src, dst, send.at[h, k], sem, device_id=dest, device_id_type=MESH
                ).start()

    def send_all(h, which, first=0, last=16):
        def body(k, carry):
            exchange(h, k, which)
            return carry

        lax.fori_loop(first, last, body, 0)

    send_all(0, (1, 2))
    send_all(0, (0,), 0, 12)
    send_all(1, (1, 2))
    send_all(0, (0,), 12, 16)
    send_all(1, (0,))

    def forward(h, k):
        dx = k % 4
        dz = (k // 4 + 4 - dx) % 4
        sx, sz = (x + 4 - dx) % 4, (z + 4 - dz) % 4

        @pl.when(sz // 2 == core)
        def _():
            for c in range(2):
                tile = sx * 2 + sz % 2
                src = kv[h].at[:, 8 + tile, pl.ds(c * HALF, HALF), :]
                pltpu.make_async_copy(src, src, kv_recv.at[h, tile * 2 + c]).wait()

                @pl.when(has_up)
                def _():
                    pltpu.make_async_remote_copy(
                        src, kv[h].at[:, tile, pl.ds(c * HALF, HALF), :],
                        fwd_send.at[h, 0], fwd_recv.at[h, 0], device_id=up_dev, device_id_type=MESH,
                    ).start()

                @pl.when(has_down)
                def _():
                    pltpu.make_async_remote_copy(
                        src, kv[h].at[:, 16 + tile, pl.ds(c * HALF, HALF), :],
                        fwd_send.at[h, 1], fwd_recv.at[h, 1], device_id=down_dev, device_id_type=MESH,
                    ).start()

    def forward_body(h, k, carry):
        forward(h, k)
        return carry

    lax.fori_loop(0, 16, functools.partial(forward_body, 0), 0)

    pltpu.make_async_copy(ints_v, ints_v, int_recv).wait()
    to_smem = pltpu.make_async_copy(ints_v, ints_s, smem_sem)
    to_smem.start()
    to_smem.wait()

    def tile_at(n):
        side = 1 - n % 2
        dx = (2 * core + side + n // 2 + 4 - z) % 4
        return ((x + 4 - dx) % 4) * 2 + side

    def query_arrived(h, a):
        pltpu.make_async_copy(q.at[h, a], q.at[h, a], q_recv.at[h, a]).wait()

    def arrived(h):
        @pl.when(has_down)
        def _():
            part = kv[h].at[:, pl.ds(0, 8)]
            pltpu.make_async_copy(part, part, fwd_recv.at[h, 0]).wait()

        @pl.when(has_up)
        def _():
            part = kv[h].at[:, pl.ds(16, 8)]
            pltpu.make_async_copy(part, part, fwd_recv.at[h, 1]).wait()

    base = 8 * (frame - 1)

    def tiles_of(a):
        return [jnp.clip(ints_s[a, s] - base, 0, 23) for s in range(NB)]

    def score(h, a, p, index, s_ref, top):
        keys = jnp.concatenate([kv[h][0, index[2 * p]], kv[h][0, index[2 * p + 1]]], axis=0)
        halves = [
            lax.dot_general(
                q[h, a, i * HALF:(i + 1) * HALF], keys, (((1,), (1,)), ((), ())), preferred_element_type=jnp.float32
            )
            for i in range(2)
        ]
        s = jnp.concatenate(halves, axis=0)
        s_ref[p] = s
        for c in range(6):
            m = s[:, c * 128:(c + 1) * 128]
            top = m if top is None else jnp.maximum(top, m)
        return top

    def keep_top(top, top_ref):
        top_ref[...] = jnp.broadcast_to(jnp.max(top, axis=1, keepdims=True), (TILE, 128))

    def blend(h, a, p, index, s_ref, row_top, rows=slice(None)):
        w = jnp.exp2((s_ref[p, rows] - row_top) * SCALE).astype(jnp.bfloat16)
        vals = []
        for s in (2 * p, 2 * p + 1):
            v = kv[h][1, index[s]]
            one = jnp.ones((TILE, 128), jnp.bfloat16)
            if s >= 6:
                live = ints_s[a, s] != ints_s[a, 0]
                v = jnp.where(live, v, jnp.zeros_like(v))
                one = jnp.where(live, one, jnp.zeros_like(one))
            vals.append(jnp.concatenate([v, one], axis=1))
        return jnp.dot(w, jnp.concatenate(vals, axis=0), preferred_element_type=jnp.float32)

    def attend(h, n, cur, nxt):
        a = tile_at(n)
        index = tiles_of(a)
        row_top = cur[1][:, 0:1]
        total, top = None, None
        if nxt is not None:
            after = tile_at(n + 1)
            query_arrived(h, after)
            index_next = tiles_of(after)
        for p in range(NB // 2):
            if nxt is not None:
                top = score(h, after, p, index_next, nxt[0], top)
            part = blend(h, a, p, index, cur[0], row_top)
            total = part if total is None else total + part
        if nxt is not None:
            keep_top(top, nxt[1])
        o[h, a] = (total[:, :128] / total[:, 128:]).astype(jnp.bfloat16)

    def o_target(a, half):
        return (y * 2 + core, 2 * a + half)

    def o_copy(h, a, half):
        col = pl.multiple_of((pair * 2 + h) * 128, 128)
        src = o.at[h, a, pl.ds(half * HALF, HALF), :]
        return src, out.at[:, pl.ds(col, 128)]

    even, odd = (s_even, top_even), (s_odd, top_odd)

    def item(h, n, cur, nxt):
        if h == 0:

            @pl.when((n >= 2) & (n <= 5))
            def _():
                start = jnp.where(n == 2, 0, 2 * n - 2)
                stop = jnp.where(n == 5, 16, 2 * n)
                lax.fori_loop(start, stop, functools.partial(forward_body, 1), 0)

        if h == 1:

            @pl.when(n < 4)
            def _():
                give(0, tile_at(2 * n))
                give(0, tile_at(2 * n + 1))

        attend(h, n, cur, nxt)
        if h == 1:
            give(1, tile_at(n))

    def give(h, a, halves=(0, 1)):
        for half in halves:
            dest = o_target(a, half)
            src, dst = o_copy(h, a, half)

            @pl.when(is_me(dest))
            def _():
                pltpu.make_async_copy(src, dst, o_recv).start()

            @pl.when(jnp.logical_not(is_me(dest)))
            def _():
                pltpu.make_async_remote_copy(
                    src, dst, o_send.at[h * 16 + a * 2 + half], o_recv, device_id=dest, device_id_type=MESH
                ).start()

    for h in range(2):
        arrived(h)
        first, top = tile_at(0), None
        query_arrived(h, first)
        index_first = tiles_of(first)
        for p in range(NB // 2):
            top = score(h, first, p, index_first, s_even, top)
        keep_top(top, top_even)

        def two(j, carry):
            item(h, 2 * j, even, odd)
            item(h, 2 * j + 1, odd, even)
            return carry

        lax.fori_loop(0, 3, two, 0)
        item(h, 6, even, odd)
        if h == 0:
            item(h, 7, odd, None)

    last = tile_at(7)
    index_last = tiles_of(last)
    for half in range(2):
        rows = slice(half * HALF, (half + 1) * HALF)
        total = None
        for p in range(NB // 2):
            part = blend(1, last, p, index_last, s_odd, top_odd[rows, 0:1], rows)
            total = part if total is None else total + part
        o[1, last, rows] = (total[:, :128] / total[:, 128:]).astype(jnp.bfloat16)
        give(1, last, (half,))

    def finish(k, carry):
        wx, wz = step_dest(k)

        @pl.when(jnp.logical_not(is_me(worker(wx, wz, y, zh))))
        def _():
            for h in range(2):
                part = q.at[h, pl.ds(0, 3), pl.ds(0, HALF), :]
                pltpu.make_async_copy(part, part, send.at[h, k]).wait()

        for half in range(2):
            a = k % 8

            @pl.when(jnp.logical_not(is_me(o_target(a, half))))
            def _():
                part = o.at[0, 0, pl.ds(0, HALF), :]
                pltpu.make_async_copy(part, part, o_send.at[k * 2 + half]).wait()

        return carry

    lax.fori_loop(0, 16, finish, 0)
    for h in range(2):
        part = kv[h].at[:, pl.ds(0, 8)]

        @pl.when(has_up)
        def _():
            pltpu.make_async_copy(part, part, fwd_send.at[h, 0]).wait()

        @pl.when(has_down)
        def _():
            pltpu.make_async_copy(part, part, fwd_send.at[h, 1]).wait()

    @pl.when(zh != core)
    def _():
        pltpu.make_async_copy(ints_v, ints_v, int_send).wait()

    pltpu.make_async_copy(out, out, o_recv).wait()


def body(queries, keys, values, neighbours, counts):
    any_space = pl.BlockSpec(memory_space=pl.ANY)
    dma = pltpu.SemaphoreType.DMA
    return settle(pl.pallas_call(
        kernel,
        out_shape=jax.ShapeDtypeStruct(queries.shape, queries.dtype),
        in_specs=[any_space] * 4,
        out_specs=any_space,
        scratch_shapes=[
            pltpu.VMEM((2, 24, TILE, HD), jnp.bfloat16),
            pltpu.VMEM((2, 24, TILE, HD), jnp.bfloat16),
            pltpu.VMEM((2, 8, TILE, HD), jnp.bfloat16),
            pltpu.VMEM((2, 8, TILE, HD), jnp.bfloat16),
            pltpu.VMEM((NB // 2, TILE, 2 * TILE), jnp.float32),
            pltpu.VMEM((NB // 2, TILE, 2 * TILE), jnp.float32),
            pltpu.VMEM((TILE, 128), jnp.float32),
            pltpu.VMEM((TILE, 128), jnp.float32),
            pltpu.VMEM((8, NB), jnp.int32),
            pltpu.SMEM((8, NB), jnp.int32),
            dma((2, 16)),
            dma((2, 8)),
            dma((2, 16)),
            dma((2, 2)),
            dma((2, 2)),
            dma((32,)),
            dma,
            dma,
            dma,
            dma,
        ],
        compiler_params=pltpu.CompilerParams(
            collective_id=0, has_side_effects=True, vmem_limit_bytes=56 * 1024 * 1024
        ),
    )(queries, keys, values, neighbours))


def settle(result):
    def copy(src, dst, held, into, outof):
        reads = [
            pltpu.make_async_copy(src.at[pl.ds(i * 48, 48)], held.at[pl.ds(i * 48, 48)], into.at[i]) for i in range(4)
        ]
        writes = [
            pltpu.make_async_copy(held.at[pl.ds(i * 48, 48)], dst.at[pl.ds(i * 48, 48)], outof.at[i]) for i in range(4)
        ]
        for c in reads:
            c.start()
        for r, c in zip(reads, writes):
            r.wait()
            c.start()
        for c in writes:
            c.wait()

    return pl.pallas_call(
        copy,
        out_shape=jax.ShapeDtypeStruct(result.shape, result.dtype),
        in_specs=[pl.BlockSpec(memory_space=pl.ANY)],
        out_specs=pl.BlockSpec(memory_space=pl.ANY),
        scratch_shapes=[
            pltpu.VMEM(result.shape, result.dtype), pltpu.SemaphoreType.DMA((4,)), pltpu.SemaphoreType.DMA((4,))
        ],
    )(result)


def solution(mesh):
    placed = (
        P(("slab", "head"), None),
        P(("slab", "head"), None),
        P(("slab", "head"), None),
        P("slab", None),
        P("slab"),
    )
    return jax.shard_map(
        body, mesh=mesh, in_specs=placed, out_specs=P(("slab", "head"), None), check_vma=False
    )
```

```python
import functools
import math

import jax
import jax.numpy as jnp
from jax import lax
from jax.experimental import pallas as pl
from jax.experimental.pallas import tpu as pltpu
from jax.sharding import PartitionSpec as P

HD = 128
TILE = 384
HALF = TILE // 2
NB = 12
MESH = pl.DeviceIdType.MESH
SCALE = math.log2(math.e) / math.sqrt(HD)


def kernel(
    q_in, k_in, v_in, ints_in, out,
    kv0, kv1, q, o, s_even, s_odd, top_even, top_odd, ints_v, ints_s,
    kv_recv, q_recv, send, fwd_recv, fwd_send, o_send, o_recv, int_recv, int_send, smem_sem,
):
    kv = (kv0, kv1)
    slab = lax.axis_index("slab")
    head = lax.axis_index("head")
    y, zh = slab // 2, slab % 2
    x, zl, core = head // 4, (head // 2) % 2, head % 2
    z = zh * 2 + zl
    frame = 2 * y + core
    pair = x * 4 + z

    def worker(wx, wz, wy, wcore):
        return (wy * 2 + wz // 2, (wx * 2 + wz % 2) * 2 + wcore)

    def is_me(where):
        return (where[0] == slab) & (where[1] == head)

    def step_dest(k):
        dx = k % 4
        dz = (k // 4 + 4 - dx) % 4
        return (x + dx) % 4, (z + dz) % 4

    up_y, up_core = (frame + 1) // 2, (frame + 1) % 2
    down_y, down_core = (frame + 1) // 2 - 1, (frame + 1) % 2
    up_dev = worker(x, z, up_y, up_core)
    down_dev = worker(x, z, down_y, down_core)
    has_up = frame < 7
    has_down = frame > 0

    barrier = pltpu.get_barrier_semaphore()

    def greet(k, count):
        wx, wz = step_dest(k)
        dest = worker(wx, wz, y, zh)
        source = (y * 2 + core, k)

        @pl.when(jnp.logical_not(is_me(dest)))
        def _():
            pl.semaphore_signal(barrier, inc=1, device_id=dest, device_id_type=MESH)

        @pl.when(jnp.logical_not(is_me(source)))
        def _():
            pl.semaphore_signal(barrier, inc=1, device_id=source, device_id_type=MESH)

        return count

    lax.fori_loop(0, 16, greet, 0)

    @pl.when(has_up)
    def _():
        pl.semaphore_signal(barrier, inc=1, device_id=up_dev, device_id_type=MESH)

    @pl.when(has_down)
    def _():
        pl.semaphore_signal(barrier, inc=1, device_id=down_dev, device_id_type=MESH)

    own = jnp.where(zh == core, 2, 0)
    pl.semaphore_wait(barrier, 32 - own + has_up.astype(jnp.int32) + has_down.astype(jnp.int32))

    partner = worker(x, core * 2 + zl, y, zh)

    @pl.when(zh == core)
    def _():
        pltpu.make_async_copy(ints_in, ints_v, int_recv).start()

    @pl.when(zh != core)
    def _():
        pltpu.make_async_remote_copy(
            ints_in, ints_v, int_send, int_recv, device_id=partner, device_id_type=MESH
        ).start()

    my_tile, my_row = head // 2, pl.multiple_of(core * HALF, HALF)

    def exchange(h, k, which):
        wx, wz = step_dest(k)
        dest = worker(wx, wz, y, zh)
        col = pl.multiple_of((wx * 4 + wz) * 256 + h * 128, 128)
        src_of = (q_in, k_in, v_in)
        for a in which:
            src = src_of[a].at[:, pl.ds(col, 128)]
            if a == 0:
                dst = q.at[h, my_tile, pl.ds(my_row, HALF), :]
                sem = q_recv.at[h, my_tile]
            else:
                dst = kv[h].at[a - 1, 8 + my_tile, pl.ds(my_row, HALF), :]
                sem = kv_recv.at[h, head]

            @pl.when(is_me(dest))
            def _():
                pltpu.make_async_copy(src, dst, sem).start()

            @pl.when(jnp.logical_not(is_me(dest)))
            def _():
                pltpu.make_async_remote_copy(
                    src, dst, send.at[h, k], sem, device_id=dest, device_id_type=MESH
                ).start()

    def send_all(h, which, first=0, last=16):
        def body(k, carry):
            exchange(h, k, which)
            return carry

        lax.fori_loop(first, last, body, 0)

    send_all(0, (1, 2))
    send_all(0, (0,), 0, 12)
    send_all(1, (1, 2))
    send_all(0, (0,), 12, 16)
    send_all(1, (0,))

    def forward(h, k):
        dx = k % 4
        dz = (k // 4 + 4 - dx) % 4
        sx, sz = (x + 4 - dx) % 4, (z + 4 - dz) % 4

        @pl.when(sz // 2 == core)
        def _():
            for c in range(2):
                tile = sx * 2 + sz % 2
                src = kv[h].at[:, 8 + tile, pl.ds(c * HALF, HALF), :]
                pltpu.make_async_copy(src, src, kv_recv.at[h, tile * 2 + c]).wait()

                @pl.when(has_up)
                def _():
                    pltpu.make_async_remote_copy(
                        src, kv[h].at[:, tile, pl.ds(c * HALF, HALF), :],
                        fwd_send.at[h, 0], fwd_recv.at[h, 0], device_id=up_dev, device_id_type=MESH,
                    ).start()

                @pl.when(has_down)
                def _():
                    pltpu.make_async_remote_copy(
                        src, kv[h].at[:, 16 + tile, pl.ds(c * HALF, HALF), :],
                        fwd_send.at[h, 1], fwd_recv.at[h, 1], device_id=down_dev, device_id_type=MESH,
                    ).start()

    def forward_body(h, k, carry):
        forward(h, k)
        return carry

    lax.fori_loop(0, 16, functools.partial(forward_body, 0), 0)

    pltpu.make_async_copy(ints_v, ints_v, int_recv).wait()
    to_smem = pltpu.make_async_copy(ints_v, ints_s, smem_sem)
    to_smem.start()
    to_smem.wait()

    def tile_at(n):
        side = 1 - n % 2
        dx = (2 * core + side + n // 2 + 4 - z) % 4
        return ((x + 4 - dx) % 4) * 2 + side

    def query_arrived(h, a):
        pltpu.make_async_copy(q.at[h, a], q.at[h, a], q_recv.at[h, a]).wait()

    def arrived(h):
        @pl.when(has_down)
        def _():
            part = kv[h].at[:, pl.ds(0, 8)]
            pltpu.make_async_copy(part, part, fwd_recv.at[h, 0]).wait()

        @pl.when(has_up)
        def _():
            part = kv[h].at[:, pl.ds(16, 8)]
            pltpu.make_async_copy(part, part, fwd_recv.at[h, 1]).wait()

    base = 8 * (frame - 1)

    def tiles_of(a):
        return [jnp.clip(ints_s[a, s] - base, 0, 23) for s in range(NB)]

    def score(h, a, p, index, s_ref, top):
        keys = jnp.concatenate([kv[h][0, index[2 * p]], kv[h][0, index[2 * p + 1]]], axis=0)
        halves = [
            lax.dot_general(
                q[h, a, i * HALF:(i + 1) * HALF], keys, (((1,), (1,)), ((), ())), preferred_element_type=jnp.float32
            )
            for i in range(2)
        ]
        s = jnp.concatenate(halves, axis=0)
        s_ref[p] = s
        for c in range(6):
            m = s[:, c * 128:(c + 1) * 128]
            top = m if top is None else jnp.maximum(top, m)
        return top

    def keep_top(top, top_ref):
        top_ref[...] = jnp.broadcast_to(jnp.max(top, axis=1, keepdims=True), (TILE, 128))

    def blend(h, a, p, index, s_ref, row_top, rows=slice(None)):
        w = jnp.exp2((s_ref[p, rows] - row_top) * SCALE).astype(jnp.bfloat16)
        vals = []
        for s in (2 * p, 2 * p + 1):
            v = kv[h][1, index[s]]
            one = jnp.ones((TILE, 128), jnp.bfloat16)
            if s >= 6:
                live = ints_s[a, s] != ints_s[a, 0]
                v = jnp.where(live, v, jnp.zeros_like(v))
                one = jnp.where(live, one, jnp.zeros_like(one))
            vals.append(jnp.concatenate([v, one], axis=1))
        return jnp.dot(w, jnp.concatenate(vals, axis=0), preferred_element_type=jnp.float32)

    def attend(h, n, cur, nxt):
        a = tile_at(n)
        index = tiles_of(a)
        row_top = cur[1][:, 0:1]
        total, top = None, None
        if nxt is not None:
            after = tile_at(n + 1)
            query_arrived(h, after)
            index_next = tiles_of(after)
        for p in range(NB // 2):
            if nxt is not None:
                top = score(h, after, p, index_next, nxt[0], top)
            part = blend(h, a, p, index, cur[0], row_top)
            total = part if total is None else total + part
        if nxt is not None:
            keep_top(top, nxt[1])
        o[h, a] = (total[:, :128] / total[:, 128:]).astype(jnp.bfloat16)

    def o_target(a, half):
        return (y * 2 + core, 2 * a + half)

    def o_copy(h, a, half):
        col = pl.multiple_of((pair * 2 + h) * 128, 128)
        src = o.at[h, a, pl.ds(half * HALF, HALF), :]
        return src, out.at[:, pl.ds(col, 128)]

    even, odd = (s_even, top_even), (s_odd, top_odd)

    def item(h, n, cur, nxt):
        if h == 0:

            @pl.when((n >= 2) & (n <= 5))
            def _():
                start = jnp.where(n == 2, 0, 2 * n - 2)
                stop = jnp.where(n == 5, 16, 2 * n)
                lax.fori_loop(start, stop, functools.partial(forward_body, 1), 0)

        if h == 1:

            @pl.when(n < 2)
            def _():
                for j in range(4):
                    give(0, tile_at(4 * n + j))

        attend(h, n, cur, nxt)
        if h == 1:
            give(1, tile_at(n))

    def give(h, a, halves=(0, 1)):
        for half in halves:
            dest = o_target(a, half)
            src, dst = o_copy(h, a, half)

            @pl.when(is_me(dest))
            def _():
                pltpu.make_async_copy(src, dst, o_recv).start()

            @pl.when(jnp.logical_not(is_me(dest)))
            def _():
                pltpu.make_async_remote_copy(
                    src, dst, o_send.at[h * 16 + a * 2 + half], o_recv, device_id=dest, device_id_type=MESH
                ).start()

    for h in range(2):
        arrived(h)
        first, top = tile_at(0), None
        query_arrived(h, first)
        index_first = tiles_of(first)
        for p in range(NB // 2):
            top = score(h, first, p, index_first, s_even, top)
        keep_top(top, top_even)

        def two(j, carry):
            item(h, 2 * j, even, odd)
            item(h, 2 * j + 1, odd, even)
            return carry

        lax.fori_loop(0, 3, two, 0)
        item(h, 6, even, odd)
        if h == 0:
            item(h, 7, odd, None)

    last = tile_at(7)
    index_last = tiles_of(last)
    for half in range(2):
        rows = slice(half * HALF, (half + 1) * HALF)
        total = None
        for p in range(NB // 2):
            part = blend(1, last, p, index_last, s_odd, top_odd[rows, 0:1], rows)
            total = part if total is None else total + part
        o[1, last, rows] = (total[:, :128] / total[:, 128:]).astype(jnp.bfloat16)
        give(1, last, (half,))

    def finish(k, carry):
        wx, wz = step_dest(k)

        @pl.when(jnp.logical_not(is_me(worker(wx, wz, y, zh))))
        def _():
            for h in range(2):
                part = q.at[h, pl.ds(0, 3), pl.ds(0, HALF), :]
                pltpu.make_async_copy(part, part, send.at[h, k]).wait()

        for half in range(2):
            a = k % 8

            @pl.when(jnp.logical_not(is_me(o_target(a, half))))
            def _():
                part = o.at[0, 0, pl.ds(0, HALF), :]
                pltpu.make_async_copy(part, part, o_send.at[k * 2 + half]).wait()

        return carry

    lax.fori_loop(0, 16, finish, 0)
    for h in range(2):
        part = kv[h].at[:, pl.ds(0, 8)]

        @pl.when(has_up)
        def _():
            pltpu.make_async_copy(part, part, fwd_send.at[h, 0]).wait()

        @pl.when(has_down)
        def _():
            pltpu.make_async_copy(part, part, fwd_send.at[h, 1]).wait()

    @pl.when(zh != core)
    def _():
        pltpu.make_async_copy(ints_v, ints_v, int_send).wait()

    pltpu.make_async_copy(out, out, o_recv).wait()


def body(queries, keys, values, neighbours, counts):
    any_space = pl.BlockSpec(memory_space=pl.ANY)
    dma = pltpu.SemaphoreType.DMA
    return settle(pl.pallas_call(
        kernel,
        out_shape=jax.ShapeDtypeStruct(queries.shape, queries.dtype),
        in_specs=[any_space] * 4,
        out_specs=any_space,
        scratch_shapes=[
            pltpu.VMEM((2, 24, TILE, HD), jnp.bfloat16),
            pltpu.VMEM((2, 24, TILE, HD), jnp.bfloat16),
            pltpu.VMEM((2, 8, TILE, HD), jnp.bfloat16),
            pltpu.VMEM((2, 8, TILE, HD), jnp.bfloat16),
            pltpu.VMEM((NB // 2, TILE, 2 * TILE), jnp.float32),
            pltpu.VMEM((NB // 2, TILE, 2 * TILE), jnp.float32),
            pltpu.VMEM((TILE, 128), jnp.float32),
            pltpu.VMEM((TILE, 128), jnp.float32),
            pltpu.VMEM((8, NB), jnp.int32),
            pltpu.SMEM((8, NB), jnp.int32),
            dma((2, 16)),
            dma((2, 8)),
            dma((2, 16)),
            dma((2, 2)),
            dma((2, 2)),
            dma((32,)),
            dma,
            dma,
            dma,
            dma,
        ],
        compiler_params=pltpu.CompilerParams(
            collective_id=0, has_side_effects=True, vmem_limit_bytes=56 * 1024 * 1024
        ),
    )(queries, keys, values, neighbours))


def settle(result):
    def copy(src, dst, held, into, outof):
        reads = [
            pltpu.make_async_copy(src.at[pl.ds(i * 48, 48)], held.at[pl.ds(i * 48, 48)], into.at[i]) for i in range(4)
        ]
        writes = [
            pltpu.make_async_copy(held.at[pl.ds(i * 48, 48)], dst.at[pl.ds(i * 48, 48)], outof.at[i]) for i in range(4)
        ]
        for c in reads:
            c.start()
        for r, c in zip(reads, writes):
            r.wait()
            c.start()
        for c in writes:
            c.wait()

    return pl.pallas_call(
        copy,
        out_shape=jax.ShapeDtypeStruct(result.shape, result.dtype),
        in_specs=[pl.BlockSpec(memory_space=pl.ANY)],
        out_specs=pl.BlockSpec(memory_space=pl.ANY),
        scratch_shapes=[
            pltpu.VMEM(result.shape, result.dtype), pltpu.SemaphoreType.DMA((4,)), pltpu.SemaphoreType.DMA((4,))
        ],
    )(result)


def solution(mesh):
    placed = (
        P(("slab", "head"), None),
        P(("slab", "head"), None),
        P(("slab", "head"), None),
        P("slab", None),
        P("slab"),
    )
    return jax.shard_map(
        body, mesh=mesh, in_specs=placed, out_specs=P(("slab", "head"), None), check_vma=False
    )
```
